128 devices in a mesh: wave: 32 (over x, y, core), lev: 4 (over z).
Axes of the slice: x: 4, y: 4, z: 4, core: 2. Of those that a mesh axis runs over, the one named last changes fastest.
Arguments:
- spec_in: bfloat16 [320, 2, 4, 128, 1281], P('wave', None, None, 'lev'), may hold values from -6 to 6
- legendre: bfloat16 [320, 1281, 256], P('wave'), may hold values from -0.15625 to 0.15625
- lat_weight: float32 [256], replicated, may hold values from 0.5 to 2
- vertical_matrix: bfloat16 [128, 128], replicated, may hold values from -0.5 to 0.5
- pair_table: int32 [320], replicated, may hold values from 0 to 639, as said below
Outputs:
- spec_out: bfloat16 [320, 2, 4, 128, 1281], P('wave', None, None, 'lev')
The draws below stay inside these ranges and needn't reach their ends.
Inputs may be any that keep to these rules, and one draw needn't show every extreme that they name: Slot s holds the wavenumbers pair_table[s] and 1279 - pair_table[s]; the values are distinct.
All inputs are finite; a program needn't handle non-finite values.
Results may differ from the reference program's by a relative error of at most 0.0075.
Values may be sent and summed in bfloat16 or wider, within the bound.
No kernel may reach another device: no remote copies, remote signals or barrier semaphores. Data moves between devices by JAX's collectives and lax.ppermute only.
A program may use at most 128 MiB of HBM per device.

```python
import math
import jax
import jax.numpy as jnp
from jax import lax

MW = 1280
NLON = 2688
FLD = 4
LEV = 128
PAIRS = 320
PLEN = 1281
NLAT = 256


def draw_pair_table(key, part):
    key = jax.random.fold_in(key, 7)
    inner_key, order_key = jax.random.split(key)
    middle = jax.random.permutation(inner_key, jnp.arange(1, MW // 2 - 1, dtype=jnp.int32))
    chosen = jnp.concatenate([jnp.array([0, MW // 2 - 1], dtype=jnp.int32), middle[:PAIRS - 2]])
    return jax.random.permutation(order_key, chosen).astype(jnp.int32)


def levels(stream_key, dims, pieces, low, high):
    gain, own = 1.0, jax.random.fold_in(stream_key, 6)
    for dim, shards_of in pieces:
        draws = jnp.exp(jax.random.uniform(jax.random.fold_in(own, dim), (shards_of,), jnp.float32, low / len(pieces), high / len(pieces)))
        gain = gain * jnp.repeat(draws, dims[dim] // shards_of).reshape([-1 if axis == dim else 1 for axis in range(len(dims))])
    return gain


def scatter_about(stream_key, shape, scale, limit, shards=(), held_as=jnp.bfloat16):
    gain = levels(stream_key, shape, shards, -0.22, 0.18) if shards else 1.0
    drawn = jax.random.normal(stream_key, shape, jnp.float32) * scale * gain
    return jnp.minimum(jnp.maximum(drawn, -limit), limit).astype(held_as)


def setup_inputs(seed: int = 0) -> dict:
    seeds = jax.random.split(jax.random.key(seed), 6)
    return {
        "spec_in": scatter_about(seeds[0], (PAIRS, 2, FLD, LEV, PLEN), 1.0, 6.0, ((0, 32), (3, 4))),
        "legendre": scatter_about(seeds[1], (PAIRS, PLEN, NLAT), PLEN ** -0.5, 0.15625, ((0, 32),)),
        "lat_weight": jnp.clip(jnp.exp(jax.random.uniform(seeds[2], (NLAT,), jnp.float32, math.log(0.5), math.log(2.0))), 0.5, 2.0),
        "vertical_matrix": scatter_about(seeds[3], (LEV, LEV), LEV ** -0.5, 0.5),
        "pair_table": draw_pair_table(jax.random.fold_in(seeds[5], 71), 0),
    }


def wave_table(pair_table, wave_count, longitudes):
    members = jnp.stack([pair_table, wave_count - 1 - pair_table], axis=1).reshape(-1)
    per_column = jnp.repeat(members, 2)
    parity = jnp.tile(jnp.arange(2, dtype=jnp.int32), members.shape[0])
    angle_index = per_column[:, None] * jnp.arange(longitudes, dtype=jnp.int32)[None, :] % longitudes
    angles = angle_index.astype(jnp.float32) * (2.0 * math.pi / longitudes)
    values = jnp.where(parity[:, None] == 0, jnp.cos(angles), -jnp.sin(angles)) / math.sqrt(wave_count)
    return values.astype(jnp.bfloat16)

def slot_layout(pair_table, wave_count, packed):
    row_index = jnp.arange(packed, dtype=jnp.int32)
    first_half = row_index[None, :] < (wave_count - pair_table)[:, None]
    degree = jnp.where(first_half, pair_table[:, None] + row_index[None, :], row_index[None, :] - 1)
    degree_real = degree.astype(jnp.float32)
    implicit = degree_real * (degree_real + 1.0) / float(wave_count * (wave_count - 1))
    return (first_half, implicit)

def reference(spec_in, legendre, lat_weight, vertical_matrix, pair_table):
    first_half, implicit = slot_layout(pair_table, MW, PLEN)

    def inverse_slot(items):
        spectral, values, chosen = items
        zeroes = jnp.zeros_like(spectral)
        halves = jnp.stack([jnp.where(chosen, spectral, zeroes), jnp.where(chosen, zeroes, spectral)])
        result = jnp.einsum('hcflr,rj->jflhc', halves.astype(jnp.float32), values.astype(jnp.float32))
        return result.astype(jnp.bfloat16)
    fourier = lax.map(inverse_slot, (spec_in, legendre, first_half))
    fourier = jnp.transpose(fourier, (1, 2, 3, 0, 4, 5)).reshape(NLAT, FLD, LEV, PAIRS * 4)
    table = wave_table(pair_table, MW, NLON)

    def grid_row(values):
        flattened = values.reshape(FLD * LEV, PAIRS * 4)
        gridded = jnp.dot(flattened, table, preferred_element_type=jnp.float32).reshape(FLD, LEV, NLON)
        tendency = (gridded + 0.5 * gridded * jnp.roll(gridded, -1, axis=0)).astype(jnp.bfloat16)
        final_output = jnp.dot(tendency.reshape(FLD * LEV, NLON), table.T, preferred_element_type=jnp.float32) * (MW / NLON)
        return final_output.astype(jnp.bfloat16).reshape(FLD, LEV, PAIRS * 4)
    final_output = lax.map(grid_row, fourier)
    linked_state = jnp.einsum('lk,jkx->jlx', vertical_matrix.astype(jnp.float32), final_output[:, 2].astype(jnp.float32)).astype(jnp.bfloat16)
    combined = jnp.concatenate([final_output, linked_state[:, None]], axis=1)
    per_slot = jnp.transpose(combined.reshape(NLAT, FLD + 1, LEV, PAIRS, 2, 2), (3, 0, 1, 2, 4, 5))
    scale = math.sqrt(PLEN / NLAT)

    def direct_slot(items):
        values, chosen, factor, gathered = items
        weighted = (values.astype(jnp.float32) * lat_weight[None, :] * scale).astype(jnp.bfloat16)
        both_halves = jnp.einsum('rj,jflhc->hcflr', weighted.astype(jnp.float32), gathered.astype(jnp.float32))
        direct = jnp.where(chosen, both_halves[0], both_halves[1])
        corrected = direct[:, 0] - factor * direct[:, FLD]
        return jnp.concatenate([corrected[:, None], direct[:, 1:FLD]], axis=1).astype(jnp.bfloat16)
    return lax.map(direct_slot, (legendre, first_half, implicit, per_slot))
```

```python
import math

import jax
import jax.numpy as jnp
from jax import lax
from jax.experimental import pallas as pl
from jax.experimental.pallas import tpu as pltpu
from jax.sharding import PartitionSpec as P

MW = 1280
NLON = 2688
FLD = 4
PLEN = 1281
NLAT = 256
SLOTS = 10
LV = 32
SRC = 32
KA = 704
KB = 768
KLAST = 672
F32 = jnp.float32
BF16 = jnp.bfloat16
VMEM_LIMIT = 56 * 1024 * 1024


def dot(a, b):
    return lax.dot_general(a, b, (((1,), (0,)), ((), ())), preferred_element_type=F32)


def dot_t(a, b):
    return lax.dot_general(a, b, (((1,), (1,)), ((), ())), preferred_element_type=F32)


def swap_matrix(outer, inner):
    n = outer * inner
    row = lax.broadcasted_iota(jnp.int32, (n, n), 0)
    col = lax.broadcasted_iota(jnp.int32, (n, n), 1)
    source = (row % outer) * inner + row // outer
    return jnp.where(col == source, 1.0, 0.0).astype(F32).astype(BF16)


def inverse_kernel(pairs, spec, leg, out, store):
    s = pl.program_id(0)
    p = pairs[s]
    edge = MW - p
    parity = p & 1
    coeff = spec[0].reshape(2 * FLD * LV, PLEN)
    rows = lax.broadcasted_iota(jnp.int32, (768, 1), 0) + 512
    first = rows < edge
    middle = leg[0, 512:1280, :]
    zero = jnp.zeros((), BF16)
    f0 = dot(coeff[:, 0:512], leg[0, 0:512, :]) + dot(
        coeff[:, 512:1280], jnp.where(first, middle, zero)
    )
    f1 = dot(coeff[:, 512:1280], jnp.where(first, zero, middle)) + coeff[:, 1280:1281].astype(
        F32
    ) * leg[0, 1280:1281, :].astype(F32)
    for h, f in enumerate((f0, f1)):
        e = jnp.bitwise_xor(parity, h)
        half = f.astype(BF16)
        for c in range(2):
            store[2 * e + c, s] = half[c * 128 : (c + 1) * 128].reshape(FLD, LV, NLAT)

    def swapped(tile, blocks):
        perm = swap_matrix(8, LV)
        for f in range(FLD):
            rows8 = blocks(f)
            moved = dot(perm, rows8).reshape(LV, 8, NLAT).astype(BF16)
            out[:, tile, :, f * NLAT : (f + 1) * NLAT] = moved

    @pl.when(s == 7)
    def _():
        for q in range(4):
            swapped(q, lambda f: store[q, 0:8, f].reshape(8 * LV, NLAT))

    @pl.when(s == 9)
    def _():
        swapped(
            4,
            lambda f: jnp.concatenate([store[q, 8 + i, f] for i in range(2) for q in range(4)], 0),
        )


def inverse_legendre(pairs, spec_in, legendre):
    return pl.pallas_call(
        inverse_kernel,
        grid=(SLOTS,),
        in_specs=[
            pl.BlockSpec(memory_space=pltpu.SMEM),
            pl.BlockSpec((1, 2, FLD, LV, PLEN), lambda s: (s, 0, 0, 0, 0)),
            pl.BlockSpec((1, PLEN, NLAT), lambda s: (s, 0, 0)),
        ],
        out_specs=pl.BlockSpec((SRC, 5, 8, FLD * NLAT), lambda s: (0, 0, 0, 0)),
        out_shape=jax.ShapeDtypeStruct((SRC, 5, 8, FLD * NLAT), BF16),
        scratch_shapes=[pltpu.VMEM((4, SLOTS, FLD, LV, NLAT), BF16)],
        compiler_params=pltpu.CompilerParams(vmem_limit_bytes=VMEM_LIMIT),
        cost_estimate=pl.CostEstimate(
            flops=6_000_000_000, bytes_accessed=17_000_000, transcendentals=0
        ),
    )(pairs, spec_in, legendre)


def small_tables(pair_table):
    pairs = pair_table.reshape(SRC, SLOTS)
    pure = pairs[:, :8].reshape(1, 256)
    mixed = jnp.repeat(pairs[:, 8:10], 4, axis=1).reshape(1, 256)
    both = jnp.broadcast_to(jnp.concatenate([pure, mixed], 1), (4, 512))
    q = jnp.arange(4, dtype=jnp.int32)[:, None]
    even_odd, part = q // 2, q % 2
    column = jnp.arange(512, dtype=jnp.int32)[None, :]
    own = (column < 256) | (column % 4 == q)
    wave = jnp.where(both % 2 == even_odd, both, MW - 1 - both)
    wave = wave.reshape(2048)
    shift = jnp.broadcast_to(part * (NLON // 4), (4, 512)).reshape(2048)
    amp = jnp.where(own, F32(1.0 / math.sqrt(MW)), F32(0.0)).reshape(2048)

    def angles(index):
        return (index % NLON).astype(F32) * F32(2.0 * math.pi / NLON)

    coarse = jnp.arange(KA // 64, dtype=jnp.int32)[:, None] * 64
    fine = jnp.arange(64, dtype=jnp.int32)[:, None]
    a1 = angles(coarse * wave[None, :])
    a2 = angles(fine * wave[None, :] + shift[None, :])
    rows = (jnp.cos(a1), jnp.sin(a1), jnp.cos(a2) * amp[None, :], jnp.sin(a2) * amp[None, :])
    coarse = jnp.arange(KB // 128, dtype=jnp.int32)[None, :] * 128
    fine = jnp.arange(128, dtype=jnp.int32)[None, :]
    b1 = angles(coarse * wave[:, None])
    b2 = angles(fine * wave[:, None] + shift[:, None])
    columns = (jnp.cos(b1), jnp.sin(b1), jnp.cos(b2) * amp[:, None], jnp.sin(b2) * amp[:, None])
    return rows, columns


def table_kernel(ca, sa, cb, sb, da, ea, db, eb, inv, direct):
    for a in range(KA // 64):
        value = ca[a : a + 1, :] * cb[...] - sa[a : a + 1, :] * sb[...]
        if a == KA // 64 - 1:
            k = lax.broadcasted_iota(jnp.int32, (64, 1), 0) + a * 64
            value = jnp.where(k <= KLAST, value, 0.0)
        inv[0, a * 64 : (a + 1) * 64, :] = value.astype(BF16)
    for a in range(KB // 128):
        value = da[:, a : a + 1] * db[...] - ea[:, a : a + 1] * eb[...]
        if a == 0 or (a + 1) * 128 > KLAST:
            k = lax.broadcasted_iota(jnp.int32, (1, 128), 1) + a * 128
            ends = (k == 0) | (k == KLAST)
            value = value * jnp.where(ends, 0.5, jnp.where(k <= KLAST, 1.0, 0.0))
        direct[0, :, a * 128 : (a + 1) * 128] = value.astype(BF16)


def wave_tables(pair_table):
    rows, columns = small_tables(pair_table)
    row_specs = [
        pl.BlockSpec((r.shape[0], 512), lambda q: (0, q)) for r in rows
    ]
    col_specs = [pl.BlockSpec((512, c.shape[1]), lambda q: (q, 0)) for c in columns]
    return pl.pallas_call(
        table_kernel,
        grid=(4,),
        in_specs=row_specs + col_specs,
        out_specs=[
            pl.BlockSpec((1, KA, 512), lambda q: (q, 0, 0)),
            pl.BlockSpec((1, 512, KB), lambda q: (q, 0, 0)),
        ],
        out_shape=[
            jax.ShapeDtypeStruct((4, KA, 512), BF16),
            jax.ShapeDtypeStruct((4, 512, KB), BF16),
        ],
        compiler_params=pltpu.CompilerParams(vmem_limit_bytes=32 * 1024 * 1024),
        cost_estimate=pl.CostEstimate(
            flops=12_000_000, bytes_accessed=9_000_000, transcendentals=0
        ),
    )(*rows, *columns)


def grid_kernel(recv, inv, direct, out2, outr, x, v):
    for t in range(5):
        tile = recv[:, t].astype(F32).reshape(256, FLD * NLAT).astype(BF16)
        if t < 4:
            x[t, 0:256, :] = tile
        else:
            for q in range(4):
                x[q, 256:512, :] = tile
    for q in range(4):
        v[q, KA:KB, :] = jnp.zeros((KB - KA, FLD * NLAT), BF16)
    step = KA // 4

    def body(i, carry):
        k = pl.ds(pl.multiple_of(i * step, 16), step)
        grids = []
        for f in range(FLD):
            lanes = slice(f * NLAT, (f + 1) * NLAT)
            ec, es, oc, os_ = [dot(inv[q, k, :], x[q, :, lanes]) for q in range(4)]
            e_plus, e_minus, o_plus, o_minus = ec + es, ec - es, oc + os_, oc - os_
            grids.append((e_plus + o_plus, e_minus + o_minus, e_plus - o_plus, e_minus - o_minus))
        for f in range(FLD):
            lanes = slice(f * NLAT, (f + 1) * NLAT)
            t0, t1, t2, t3 = [
                g + 0.5 * g * n for g, n in zip(grids[f], grids[(f + 1) % FLD])
            ]
            e_plus, o_plus, e_minus, o_minus = t0 + t2, t0 - t2, t1 + t3, t1 - t3
            v[0, k, lanes] = (e_plus + e_minus).astype(BF16)
            v[1, k, lanes] = (e_plus - e_minus).astype(BF16)
            v[2, k, lanes] = (o_plus + o_minus).astype(BF16)
            v[3, k, lanes] = (o_plus - o_minus).astype(BF16)
        return carry

    lax.fori_loop(0, 4, body, 0)
    scale = MW / NLON

    def put(f, tile, value):
        value = (value * scale).reshape(SRC, 8, NLAT).astype(BF16)
        if f == 2:
            out2[:, tile] = value
        else:
            place = {0: 0, 1: 1, 3: 2}[f]
            outr[:, tile, :, place * NLAT : (place + 1) * NLAT] = value

    for f in range(FLD):
        lanes = slice(f * NLAT, (f + 1) * NLAT)
        mixed = None
        for q in range(4):
            put(f, q, dot(direct[q, 0:256, :], v[q, :, lanes]))
            term = dot(direct[q, 256:512, :], v[q, :, lanes])
            mixed = term if mixed is None else mixed + term
        put(f, 4, mixed)


def grid_step(received, inv, direct):
    return pl.pallas_call(
        grid_kernel,
        out_shape=[
            jax.ShapeDtypeStruct((SRC, 5, 8, NLAT), BF16),
            jax.ShapeDtypeStruct((SRC, 5, 8, 3 * NLAT), BF16),
        ],
        scratch_shapes=[
            pltpu.VMEM((4, 512, FLD * NLAT), BF16),
            pltpu.VMEM((4, KB, FLD * NLAT), BF16),
        ],
        compiler_params=pltpu.CompilerParams(vmem_limit_bytes=VMEM_LIMIT),
        cost_estimate=pl.CostEstimate(
            flops=7_000_000_000, bytes_accessed=12_000_000, transcendentals=0
        ),
    )(received, inv, direct)


def unswap(recv, lanes, write):
    perm = swap_matrix(LV, 8)
    for t in range(5):
        tile = recv[:, t, :, lanes].astype(F32).reshape(8 * LV, NLAT).astype(BF16)
        moved = dot(perm, tile).astype(BF16).reshape(8, LV, NLAT)
        for r in range(8):
            if t < 4:
                write(t, r, moved[r])
            else:
                write(r % 4, 8 + r // 4, moved[r])


def thermal_kernel(recv, out):
    def write(q, s, value):
        out[q, s] = value

    unswap(recv, slice(0, NLAT), write)


def thermal_rows(received):
    return pl.pallas_call(
        thermal_kernel,
        out_shape=jax.ShapeDtypeStruct((4, SLOTS, LV, NLAT), BF16),
        compiler_params=pltpu.CompilerParams(vmem_limit_bytes=16 * 1024 * 1024),
        cost_estimate=pl.CostEstimate(
            flops=170_000_000, bytes_accessed=1_400_000, transcendentals=0
        ),
    )(received)


def link_kernel(matrix, r0, r1, r2, r3, o0, o1, o2, o3):
    for s in range(SLOTS):
        column = jnp.concatenate([r[s] for r in (r0, r1, r2, r3)], 0)
        result = dot(matrix[...], column).astype(BF16)
        for i, o in enumerate((o0, o1, o2, o3)):
            o[s] = result[i * LV : (i + 1) * LV]


def vertical_link(rows, vertical_matrix):
    me = lax.axis_index("lev")
    double = jnp.concatenate([vertical_matrix, vertical_matrix], 0)
    rolled = lax.dynamic_slice_in_dim(double, me * LV, 4 * LV, 0)
    double = jnp.concatenate([rolled, rolled], 1)
    rolled = lax.dynamic_slice_in_dim(double, me * LV, 4 * LV, 1)

    def moved(value, shift):
        if shift == 0:
            return value
        return lax.ppermute(value, "lev", [(i, (i + shift) % 4) for i in range(4)])

    def chunk(shift):
        return lax.dynamic_index_in_dim(rows, (me + shift) % 4, 0, keepdims=False)

    order = (1, 3, 2, 0)
    got = {shift: moved(chunk(shift), shift) for shift in order}
    relative = [got[(-i) % 4] for i in range(4)]
    shape = jax.ShapeDtypeStruct((SLOTS, LV, NLAT), BF16)
    linked = pl.pallas_call(
        link_kernel,
        out_shape=[shape] * 4,
        compiler_params=pltpu.CompilerParams(vmem_limit_bytes=16 * 1024 * 1024),
        cost_estimate=pl.CostEstimate(
            flops=90_000_000, bytes_accessed=1_400_000, transcendentals=0
        ),
    )(rolled, *relative)
    back = {shift: moved(linked[shift], shift) for shift in order}
    return [back[shift] for shift in range(4)]


def direct_kernel(scalars, recv, rows2, c0, c1, c2, c3, leg, weight, out, store, coupled):
    s = pl.program_id(0)

    @pl.when(s == 0)
    def _():
        me = scalars[SLOTS]
        for shift, c in enumerate((c0, c1, c2, c3)):
            coupled[lax.rem(me - shift + 4, 4)] = c[...]
        for place in range(3):
            def write(q, slot, value):
                store[place, q, slot] = value

            unswap(recv, slice(place * NLAT, (place + 1) * NLAT), write)

    p = scalars[s]
    edge = MW - p
    parity = p & 1
    weighted = (leg[0].astype(F32) * weight[...] * math.sqrt(PLEN / NLAT)).astype(BF16)

    def left(h):
        e = jnp.bitwise_xor(parity, h)
        blocks = []
        for c in range(2):
            q = 2 * e + c
            blocks += [
                store[0, q, s], store[1, q, s], rows2[q, s], store[2, q, s], coupled[q, s]
            ]
        return jnp.concatenate(blocks, 0)

    l0, l1 = left(0), left(1)

    def finish(value, r0, width):
        r = lax.broadcasted_iota(jnp.int32, (1, width), 1) + r0
        degree = jnp.where(r < edge, p + r, r - 1).astype(F32)
        implicit = degree * (degree + 1.0) / float(MW * (MW - 1))
        value = value.reshape(2, FLD + 1, LV, width)
        for c in range(2):
            out[0, c, 0, :, r0 : r0 + width] = (
                value[c, 0] - implicit * value[c, 4]
            ).astype(BF16)
            for f in range(1, FLD):
                out[0, c, f, :, r0 : r0 + width] = value[c, f].astype(BF16)

    for r0 in range(0, 1280, 256):
        w = weighted[r0 : r0 + 256]
        value = dot_t(l0, w)
        if r0 >= 512:
            r = lax.broadcasted_iota(jnp.int32, (1, 256), 1) + r0
            value = jnp.where(r < edge, value, dot_t(l1, w))
        finish(value, r0, 256)
    last = jnp.sum(
        l1.astype(F32) * weighted[1280:1281].astype(F32), axis=1, keepdims=True
    )
    finish(last, 1280, 1)


def direct_legendre(scalars, received, rows2, coupled, legendre, lat_weight):
    whole = lambda a: pl.BlockSpec(a.shape, lambda s: (0,) * a.ndim)
    return pl.pallas_call(
        direct_kernel,
        grid=(SLOTS,),
        in_specs=[pl.BlockSpec(memory_space=pltpu.SMEM), whole(received), whole(rows2)]
        + [whole(c) for c in coupled]
        + [pl.BlockSpec((1, PLEN, NLAT), lambda s: (s, 0, 0)), whole(lat_weight)],
        out_specs=pl.BlockSpec((1, 2, FLD, LV, PLEN), lambda s: (s, 0, 0, 0, 0)),
        out_shape=jax.ShapeDtypeStruct((SLOTS, 2, FLD, LV, PLEN), BF16),
        scratch_shapes=[
            pltpu.VMEM((3, 4, SLOTS, LV, NLAT), BF16),
            pltpu.VMEM((4, SLOTS, LV, NLAT), BF16),
        ],
        compiler_params=pltpu.CompilerParams(vmem_limit_bytes=VMEM_LIMIT),
        cost_estimate=pl.CostEstimate(
            flops=7_000_000_000, bytes_accessed=17_000_000, transcendentals=0
        ),
    )(scalars, received, rows2, *coupled, legendre, lat_weight)


def exchange(value):
    return lax.all_to_all(value, "wave", split_axis=0, concat_axis=0, tiled=True)


def local(spec_in, legendre, lat_weight, vertical_matrix, pair_table):
    pairs = lax.dynamic_slice_in_dim(pair_table, lax.axis_index("wave") * SLOTS, SLOTS)
    sent = inverse_legendre(pairs, spec_in, legendre)
    received = exchange(sent)
    inv, direct = wave_tables(pair_table)
    back2, back_rest = grid_step(received, inv, direct)
    arrived2 = exchange(back2)
    arrived_rest = exchange(back_rest)
    rows2 = thermal_rows(arrived2)
    coupled = vertical_link(rows2, vertical_matrix)
    scalars = jnp.concatenate([pairs, lax.axis_index("lev").reshape(1)]).astype(jnp.int32)
    return direct_legendre(
        scalars, arrived_rest, rows2, coupled, legendre, lat_weight.reshape(1, NLAT)
    )


def solution(mesh):
    return jax.shard_map(
        local,
        mesh=mesh,
        in_specs=(P("wave", None, None, "lev", None), P("wave", None, None), P(), P(), P()),
        out_specs=P("wave", None, None, "lev", None),
        check_vma=False,
    )
```

```python
import functools
import math

import jax
import jax.numpy as jnp
from jax import lax
from jax.experimental import pallas as pl
from jax.experimental.pallas import tpu as pltpu
from jax.sharding import PartitionSpec as P

MW = 1280
NLON = 2688
FLD = 4
PLEN = 1281
NLAT = 256
SLOTS = 10
LV = 32
SRC = 32
KA = 704
KB = 768
KLAST = 672
F32 = jnp.float32
BF16 = jnp.bfloat16
MIB = 1024 * 1024
VM = pl.BlockSpec(memory_space=pltpu.VMEM)


def in_hbm(a):
    return pltpu.with_memory_space_constraint(a, pltpu.HBM)


def dot(a, b):
    return lax.dot_general(a, b, (((1,), (0,)), ((), ())), preferred_element_type=F32)


def dot_t(a, b):
    return lax.dot_general(a, b, (((1,), (1,)), ((), ())), preferred_element_type=F32)


def swap_matrix(outer, inner):
    n = outer * inner
    row = lax.broadcasted_iota(jnp.int32, (n, n), 0)
    col = lax.broadcasted_iota(jnp.int32, (n, n), 1)
    source = (row % outer) * inner + row // outer
    return jnp.where(col == source, 1.0, 0.0).astype(F32).astype(BF16)


def inverse_kernel(pairs, spec, leg, out, coeffs, legs, store, moved, sem, out_sem):
    base = lax.axis_index("wave") * SLOTS
    window = 5

    def copies(s):
        return (
            pltpu.make_async_copy(spec.at[s], coeffs.at[s], sem.at[0, s]),
            pltpu.make_async_copy(leg.at[s], legs.at[s], sem.at[1, s]),
        )

    def start(s):
        for copy in copies(s):
            copy.start()

    for s in range(window):
        start(s)

    def step(s, carry):
        @pl.when(s + window < SLOTS)
        def _():
            start(s + window)

        for copy in copies(s):
            copy.wait()
        p = pairs[base + s]
        edge = MW - p
        parity = p & 1
        coeff = coeffs[s].reshape(2 * FLD * LV, PLEN)
        column = lax.broadcasted_iota(jnp.int32, (1, 768), 1) + 512
        first = jnp.where(column < edge, 1.0, 0.0).astype(BF16)
        second = jnp.where(column < edge, 0.0, 1.0).astype(BF16)
        middle = coeff[:, 512:1280]
        both = dot(
            jnp.concatenate([middle * first, middle * second], 0), legs[s, 512:1280, :]
        )
        last = coeff[:, 1280:1281].astype(F32) * legs[s, 1280:1281, :].astype(F32)
        halves = (both[:256] + dot(coeff[:, 0:512], legs[s, 0:512, :]), both[256:] + last)
        for h in range(2):
            e = jnp.bitwise_xor(parity, h)
            half = halves[h].astype(BF16)
            for c in range(2):
                store[2 * e + c, s] = half[c * 128 : (c + 1) * 128].reshape(FLD, LV, NLAT)
        return carry

    perm = swap_matrix(8, LV)
    leave = [
        pltpu.make_async_copy(moved.at[t], out.at[:, t], out_sem.at[t]) for t in range(5)
    ]

    def swapped(tile, blocks):
        for f in range(FLD):
            value = dot(perm, blocks(f)).reshape(LV, 8, NLAT).astype(BF16)
            moved[tile, :, :, f * NLAT : (f + 1) * NLAT] = value
        leave[tile].start()

    lax.fori_loop(0, 8, step, 0)
    for q in range(4):
        swapped(q, lambda f: store[q, 0:8, f].reshape(8 * LV, NLAT))
    lax.fori_loop(8, SLOTS, step, 0)
    swapped(
        4, lambda f: jnp.concatenate([store[q, 8 + i, f] for i in range(2) for q in range(4)], 0)
    )
    for t in range(5):
        leave[t].wait()


def inverse_legendre(pair_table, spec_in, legendre):
    return pl.pallas_call(
        inverse_kernel,
        in_specs=[pl.BlockSpec(memory_space=pltpu.SMEM)]
        + [pl.BlockSpec(memory_space=pl.ANY)] * 2,
        out_specs=pl.BlockSpec(memory_space=pl.ANY),
        out_shape=pltpu.HBM((SRC, 5, 8, FLD * NLAT), BF16),
        scratch_shapes=[
            pltpu.VMEM((SLOTS, 2, FLD, LV, PLEN), BF16),
            pltpu.VMEM((SLOTS, PLEN, NLAT), BF16),
            pltpu.VMEM((4, SLOTS, FLD, LV, NLAT), BF16),
            pltpu.VMEM((5, SRC, 8, FLD * NLAT), BF16),
            pltpu.SemaphoreType.DMA((2, SLOTS)),
            pltpu.SemaphoreType.DMA((5,)),
        ],
        compiler_params=pltpu.CompilerParams(vmem_limit_bytes=32 * MIB),
        cost_estimate=pl.CostEstimate(
            flops=6_000_000_000, bytes_accessed=17_000_000, transcendentals=0
        ),
    )(in_hbm(pair_table), in_hbm(spec_in), in_hbm(legendre))


def small_tables(pair_table):
    pairs = pair_table.reshape(SRC, SLOTS)
    pure = pairs[:, :8].reshape(1, 256)
    mixed = jnp.repeat(pairs[:, 8:10], 4, axis=1).reshape(1, 256)
    both = jnp.broadcast_to(jnp.concatenate([pure, mixed], 1), (4, 512))
    q = jnp.arange(4, dtype=jnp.int32)[:, None]
    even_odd, part = q // 2, q % 2
    column = jnp.arange(512, dtype=jnp.int32)[None, :]
    own = (column < 256) | (column % 4 == q)
    wave = jnp.where(both % 2 == even_odd, both, MW - 1 - both)
    wave = wave.reshape(2048)
    shift = jnp.broadcast_to(part * (NLON // 4), (4, 512)).reshape(2048)
    amp = jnp.where(own, F32(1.0 / math.sqrt(MW)), F32(0.0)).reshape(2048)

    def angles(index):
        return (index % NLON).astype(F32) * F32(2.0 * math.pi / NLON)

    coarse = jnp.arange(KA // 64, dtype=jnp.int32)[:, None] * 64
    fine = jnp.arange(64, dtype=jnp.int32)[:, None]
    a1 = angles(coarse * wave[None, :])
    a2 = angles(fine * wave[None, :] + shift[None, :])
    rows = (jnp.cos(a1), jnp.sin(a1), jnp.cos(a2) * amp[None, :], jnp.sin(a2) * amp[None, :])
    coarse = jnp.arange(KB // 128, dtype=jnp.int32)[None, :] * 128
    fine = jnp.arange(128, dtype=jnp.int32)[None, :]
    b1 = angles(coarse * wave[:, None])
    b2 = angles(fine * wave[:, None] + shift[:, None])
    columns = (jnp.cos(b1), jnp.sin(b1), jnp.cos(b2) * amp[:, None], jnp.sin(b2) * amp[:, None])
    return rows, columns


def table_kernel(ca, sa, cb, sb, da, ea, db, eb, leg, weight, inv, direct, weighted):
    weighted[0] = (leg[0].astype(F32) * weight[...] * math.sqrt(PLEN / NLAT)).astype(BF16)

    @pl.when(pl.program_id(0) < 4)
    def _():
        for a in range(KA // 64):
            value = ca[a : a + 1, :] * cb[...] - sa[a : a + 1, :] * sb[...]
            if a == KA // 64 - 1:
                k = lax.broadcasted_iota(jnp.int32, (64, 1), 0) + a * 64
                value = jnp.where(k <= KLAST, value, 0.0)
            inv[0, a * 64 : (a + 1) * 64, :] = value.astype(BF16)
        for a in range(KB // 128):
            value = da[:, a : a + 1] * db[...] - ea[:, a : a + 1] * eb[...]
            if a == 0 or (a + 1) * 128 > KLAST:
                k = lax.broadcasted_iota(jnp.int32, (1, 128), 1) + a * 128
                ends = (k == 0) | (k == KLAST)
                value = value * jnp.where(ends, 0.5, jnp.where(k <= KLAST, 1.0, 0.0))
            direct[0, :, a * 128 : (a + 1) * 128] = value.astype(BF16)


def all_tables(pair_table, legendre, lat_weight):
    rows, columns = small_tables(pair_table)
    group = lambda s: jnp.minimum(s, 3)
    row_specs = [pl.BlockSpec((r.shape[0], 512), lambda s: (0, group(s))) for r in rows]
    col_specs = [pl.BlockSpec((512, c.shape[1]), lambda s: (group(s), 0)) for c in columns]
    slot_spec = pl.BlockSpec((1, PLEN, NLAT), lambda s: (s, 0, 0))
    return pl.pallas_call(
        table_kernel,
        grid=(SLOTS,),
        in_specs=row_specs
        + col_specs
        + [slot_spec, pl.BlockSpec((1, NLAT), lambda s: (0, 0))],
        out_specs=[
            pl.BlockSpec((1, KA, 512), lambda s: (group(s), 0, 0)),
            pl.BlockSpec((1, 512, KB), lambda s: (group(s), 0, 0)),
            slot_spec,
        ],
        out_shape=[
            pltpu.HBM((4, KA, 512), BF16),
            pltpu.HBM((4, 512, KB), BF16),
            pltpu.HBM((SLOTS, PLEN, NLAT), BF16),
        ],
        compiler_params=pltpu.CompilerParams(vmem_limit_bytes=24 * MIB),
        cost_estimate=pl.CostEstimate(
            flops=20_000_000, bytes_accessed=26_000_000, transcendentals=0
        ),
    )(*rows, *columns, in_hbm(legendre), lat_weight.reshape(1, NLAT))


def grid_kernel(needed, wanted, recv, inv_any, direct_any, out, inv, direct, x, v, sem):
    get_inv = [
        pltpu.make_async_copy(inv_any.at[q], inv.at[q], sem.at[0, q]) for q in range(4)
    ]
    get_direct = [
        pltpu.make_async_copy(direct_any.at[q], direct.at[q], sem.at[1, q]) for q in range(4)
    ]
    for copy in get_inv + get_direct:
        copy.start()
    for t in range(5):
        for i in range(len(needed)):
            lanes = slice(i * NLAT, (i + 1) * NLAT)
            f = needed[i]
            tile = recv[:, t, :, f * NLAT : (f + 1) * NLAT].astype(F32)
            tile = tile.reshape(256, NLAT).astype(BF16)
            for q in range(4) if t == 4 else (t,):
                row = 256 if t == 4 else 0
                x[q, row : row + 256, lanes] = tile
    sums = {}
    for q in range(4):
        get_inv[q].wait()
        for i, f in enumerate(needed):
            sums[f, q] = dot(inv[q], x[q, :, i * NLAT : (i + 1) * NLAT])
    grids = {}
    for f in needed:
        ec, es, oc, os_ = [sums[f, q] for q in range(4)]
        e_plus, e_minus, o_plus, o_minus = ec + es, ec - es, oc + os_, oc - os_
        grids[f] = (e_plus + o_plus, e_minus + o_minus, e_plus - o_plus, e_minus - o_minus)
    for q in range(4):
        get_direct[q].wait()
    scale = MW / NLON
    for i, f in enumerate(wanted):
        lanes = slice(i * NLAT, (i + 1) * NLAT)
        t0, t1, t2, t3 = [g + 0.5 * g * n for g, n in zip(grids[f], grids[(f + 1) % FLD])]
        e_plus, o_plus, e_minus, o_minus = t0 + t2, t0 - t2, t1 + t3, t1 - t3
        v[0, 0:KA, lanes] = (e_plus + e_minus).astype(BF16)
        v[1, 0:KA, lanes] = (e_plus - e_minus).astype(BF16)
        v[2, 0:KA, lanes] = (o_plus + o_minus).astype(BF16)
        v[3, 0:KA, lanes] = (o_plus - o_minus).astype(BF16)
        mixed = None
        for q in range(4):
            v[q, KA:KB, lanes] = jnp.zeros((KB - KA, NLAT), BF16)
            pure = dot(direct[q, 0:256, :], v[q, :, lanes]) * scale
            out[:, q, :, lanes] = pure.reshape(SRC, 8, NLAT).astype(BF16)
            term = dot(direct[q, 256:512, :], v[q, :, lanes])
            mixed = term if mixed is None else mixed + term
        out[:, 4, :, lanes] = (mixed * scale).reshape(SRC, 8, NLAT).astype(BF16)


def grid_step(needed, wanted, received, inv, direct):
    return pl.pallas_call(
        functools.partial(grid_kernel, needed, wanted),
        in_specs=[VM] + [pl.BlockSpec(memory_space=pl.ANY)] * 2,
        out_specs=VM,
        out_shape=pltpu.HBM((SRC, 5, 8, len(wanted) * NLAT), BF16),
        scratch_shapes=[
            pltpu.VMEM((4, KA, 512), BF16),
            pltpu.VMEM((4, 512, KB), BF16),
            pltpu.VMEM((4, 512, len(needed) * NLAT), BF16),
            pltpu.VMEM((4, KB, len(wanted) * NLAT), BF16),
            pltpu.SemaphoreType.DMA((2, 4)),
        ],
        compiler_params=pltpu.CompilerParams(vmem_limit_bytes=(12 + 8 * len(wanted)) * MIB),
        cost_estimate=pl.CostEstimate(
            flops=2_000_000_000 * len(wanted), bytes_accessed=9_000_000, transcendentals=0
        ),
    )(received, in_hbm(inv), in_hbm(direct))


def unswap(recv, lanes, write):
    perm = swap_matrix(LV, 8)
    for t in range(5):
        tile = recv[:, t, :, lanes].astype(F32).reshape(8 * LV, NLAT).astype(BF16)
        moved = dot(perm, tile).astype(BF16).reshape(8, LV, NLAT)
        for r in range(8):
            if t < 4:
                write(t, r, moved[r])
            else:
                write(r % 4, 8 + r // 4, moved[r])


def thermal_kernel(recv, out):
    def write(q, s, value):
        out[q, s] = value

    unswap(recv, slice(0, NLAT), write)


def thermal_rows(received):
    return pl.pallas_call(
        thermal_kernel,
        out_shape=jax.ShapeDtypeStruct((4, SLOTS, LV, NLAT), BF16),
        compiler_params=pltpu.CompilerParams(vmem_limit_bytes=16 * MIB),
        cost_estimate=pl.CostEstimate(
            flops=170_000_000, bytes_accessed=1_400_000, transcendentals=0
        ),
    )(received)


def link_kernel(matrix, r0, r1, r2, r3, o0, o1, o2, o3):
    for s in range(SLOTS):
        column = jnp.concatenate([r[s] for r in (r0, r1, r2, r3)], 0)
        result = dot(matrix[...], column).astype(BF16)
        for i, o in enumerate((o0, o1, o2, o3)):
            o[s] = result[i * LV : (i + 1) * LV]


def vertical_link(rows, vertical_matrix):
    me = lax.axis_index("lev")
    double = jnp.concatenate([vertical_matrix, vertical_matrix], 0)
    rolled = lax.dynamic_slice_in_dim(double, me * LV, 4 * LV, 0)
    double = jnp.concatenate([rolled, rolled], 1)
    rolled = lax.dynamic_slice_in_dim(double, me * LV, 4 * LV, 1)

    def moved(value, shift):
        if shift == 0:
            return value
        return lax.ppermute(value, "lev", [(i, (i + shift) % 4) for i in range(4)])

    def chunk(shift):
        return lax.dynamic_index_in_dim(rows, (me + shift) % 4, 0, keepdims=False)

    order = (1, 3, 2, 0)
    got = {shift: moved(chunk(shift), shift) for shift in order}
    relative = [got[(-i) % 4] for i in range(4)]
    shape = jax.ShapeDtypeStruct((SLOTS, LV, NLAT), BF16)
    linked = pl.pallas_call(
        link_kernel,
        out_shape=[shape] * 4,
        compiler_params=pltpu.CompilerParams(vmem_limit_bytes=16 * MIB),
        cost_estimate=pl.CostEstimate(
            flops=90_000_000, bytes_accessed=1_400_000, transcendentals=0
        ),
    )(rolled, *relative)
    back = {shift: moved(linked[shift], shift) for shift in order}
    return [back[shift] for shift in range(4)]


def edge_of(pairs, s):
    p = pairs[lax.axis_index("wave") * SLOTS + s]
    return p, MW - p, p & 1


def legendre_rows(edge, left, weighted, give, mend):
    for r0 in range(0, 1280, 256):
        half = 0 if r0 < 512 else (r0 >= edge).astype(jnp.int32)
        give(r0, 256, dot_t(left(half), weighted(r0, 256)))
    left1 = left(1)
    row = weighted(1280, 1).astype(F32)
    give(1280, 1, jnp.sum(left1.astype(F32) * row, axis=1, keepdims=True))
    r0 = pl.multiple_of(jnp.minimum(edge // 256, 4) * 256, 256)
    r = lax.broadcasted_iota(jnp.int32, (1, 256), 1) + r0
    mend(r0, r < edge, dot_t(left1, weighted(r0, 256)))


def over_slots(weight, table, sem, before, slot, leave):
    window = 4

    def arrive(s):
        return pltpu.make_async_copy(weight.at[s], table.at[s], sem.at[s])

    for s in range(window):
        arrive(s).start()
    before()

    def step(s, carry):
        @pl.when(s + window < SLOTS)
        def _():
            arrive(s + window).start()

        arrive(s).wait()
        slot(s, lambda r0, width: table[s, pl.ds(r0, width), :])
        for copy in leave(s):
            copy.start()
        return carry

    lax.fori_loop(0, SLOTS, step, 0)
    for s in range(SLOTS):
        for copy in leave(s):
            copy.wait()


def thermal_result_kernel(pairs, rows2, weight, out, table, stage, sem, out_sem):
    def leave(s):
        return [
            pltpu.make_async_copy(stage.at[s, c], out.at[s, c, 2], out_sem.at[s, c])
            for c in range(2)
        ]

    def slot(s, weighted):
        p, edge, parity = edge_of(pairs, s)

        def left(h):
            q = 2 * jnp.bitwise_xor(parity, h)
            return jnp.concatenate([rows2[q, s], rows2[q + 1, s]], 0)

        def give(r0, width, value):
            value = value.reshape(2, LV, width).astype(BF16)
            stage[s, :, :, r0 : r0 + width] = value

        def mend(r0, keep, value):
            lanes = pl.ds(r0, 256)
            value = jnp.where(keep, stage[s, :, :, lanes].astype(F32), value.reshape(2, LV, 256))
            stage[s, :, :, lanes] = value.astype(BF16)

        legendre_rows(edge, left, weighted, give, mend)

    over_slots(weight, table, sem, lambda: None, slot, leave)


def thermal_result(pair_table, rows2, weighted):
    return pl.pallas_call(
        thermal_result_kernel,
        in_specs=[
            pl.BlockSpec(memory_space=pltpu.SMEM), VM, pl.BlockSpec(memory_space=pl.ANY)
        ],
        out_specs=pl.BlockSpec(memory_space=pl.ANY),
        out_shape=jax.ShapeDtypeStruct((SLOTS, 2, FLD, LV, PLEN), BF16),
        scratch_shapes=[
            pltpu.VMEM((SLOTS, PLEN, NLAT), BF16),
            pltpu.VMEM((SLOTS, 2, LV, PLEN), BF16),
            pltpu.SemaphoreType.DMA((SLOTS,)),
            pltpu.SemaphoreType.DMA((SLOTS, 2)),
        ],
        compiler_params=pltpu.CompilerParams(vmem_limit_bytes=20 * MIB),
        cost_estimate=pl.CostEstimate(
            flops=2_000_000_000, bytes_accessed=9_000_000, transcendentals=0
        ),
    )(pair_table, rows2, in_hbm(weighted))


def rest_kernel(pairs, recv, c0, c1, c2, c3, weight, begun, out, store, table, stage, sem, out_sem):
    def before():
        me = lax.axis_index("lev")
        for shift, c in enumerate((c0, c1, c2, c3)):
            store[3, lax.rem(me - shift + 4, 4)] = c[...]
        for place in range(3):
            def write(q, slot, value):
                store[place, q, slot] = value

            unswap(recv, slice(place * NLAT, (place + 1) * NLAT), write)

    def leave(s):
        return [
            pltpu.make_async_copy(
                stage.at[s, c, pl.ds(0, 2)], out.at[s, c, pl.ds(0, 2)], out_sem.at[s, c, 0]
            )
            for c in range(2)
        ] + [
            pltpu.make_async_copy(stage.at[s, c, 2], out.at[s, c, 3], out_sem.at[s, c, 1])
            for c in range(2)
        ]

    def slot(s, weighted):
        p, edge, parity = edge_of(pairs, s)

        def left(h):
            q = 2 * jnp.bitwise_xor(parity, h)
            return jnp.concatenate([store[f, q + c, s] for c in range(2) for f in range(4)], 0)

        def corrected(r0, width, value):
            r = lax.broadcasted_iota(jnp.int32, (1, width), 1) + r0
            degree = jnp.where(r < edge, p + r, r - 1).astype(F32)
            implicit = degree * (degree + 1.0) / float(MW * (MW - 1))
            value = value.reshape(2, 4, LV, width)
            return [
                [value[c, 0] - implicit * value[c, 3], value[c, 1], value[c, 2]] for c in range(2)
            ]

        def give(r0, width, value):
            for c, fields in enumerate(corrected(r0, width, value)):
                for f in range(3):
                    stage[s, c, f, :, r0 : r0 + width] = fields[f].astype(BF16)

        def mend(r0, keep, value):
            lanes = pl.ds(r0, 256)
            for c, fields in enumerate(corrected(r0, 256, value)):
                for f in range(3):
                    kept = stage[s, c, f, :, lanes].astype(F32)
                    stage[s, c, f, :, lanes] = jnp.where(keep, kept, fields[f]).astype(BF16)

        legendre_rows(edge, left, weighted, give, mend)

    over_slots(weight, table, sem, before, slot, leave)


def rest_result(pair_table, received, coupled, weighted, begun):
    return pl.pallas_call(
        rest_kernel,
        in_specs=[pl.BlockSpec(memory_space=pltpu.SMEM)]
        + [VM] * 5
        + [pl.BlockSpec(memory_space=pl.ANY)] * 2,
        out_specs=pl.BlockSpec(memory_space=pl.ANY),
        out_shape=jax.ShapeDtypeStruct((SLOTS, 2, FLD, LV, PLEN), BF16),
        input_output_aliases={7: 0},
        scratch_shapes=[
            pltpu.VMEM((4, 4, SLOTS, LV, NLAT), BF16),
            pltpu.VMEM((SLOTS, PLEN, NLAT), BF16),
            pltpu.VMEM((SLOTS, 2, 3, LV, PLEN), BF16),
            pltpu.SemaphoreType.DMA((SLOTS,)),
            pltpu.SemaphoreType.DMA((SLOTS, 2, 2)),
        ],
        compiler_params=pltpu.CompilerParams(vmem_limit_bytes=24 * MIB),
        cost_estimate=pl.CostEstimate(
            flops=5_000_000_000, bytes_accessed=15_000_000, transcendentals=0
        ),
    )(pair_table, received, *coupled, in_hbm(weighted), in_hbm(begun))


def exchange(value):
    return lax.all_to_all(value, "wave", split_axis=0, concat_axis=0, tiled=True)


def local(spec_in, legendre, lat_weight, vertical_matrix, pair_table):
    sent = inverse_legendre(pair_table, spec_in, legendre)
    received = exchange(sent)
    inv, direct, weighted = all_tables(pair_table, legendre, lat_weight)
    arrived2 = exchange(grid_step((2, 3), (2,), received, inv, direct))
    arrived_rest = exchange(grid_step((0, 1, 2, 3), (0, 1, 3), received, inv, direct))
    rows2 = thermal_rows(arrived2)
    coupled = vertical_link(rows2, vertical_matrix)
    begun = thermal_result(pair_table, rows2, weighted)
    return rest_result(pair_table, arrived_rest, coupled, weighted, begun)


def solution(mesh):
    return jax.shard_map(
        local,
        mesh=mesh,
        in_specs=(P("wave", None, None, "lev", None), P("wave", None, None), P(), P(), P()),
        out_specs=P("wave", None, None, "lev", None),
        check_vma=False,
    )
```

```python
import functools
import math

import jax
import jax.numpy as jnp
from jax import lax
from jax.experimental import pallas as pl
from jax.experimental.pallas import tpu as pltpu
from jax.sharding import PartitionSpec as P

MW = 1280
NLON = 2688
FLD = 4
PLEN = 1281
NLAT = 256
SLOTS = 10
LV = 32
SRC = 32
KA = 704
KB = 768
KLAST = 672
F32 = jnp.float32
BF16 = jnp.bfloat16
MIB = 1024 * 1024
VM = pl.BlockSpec(memory_space=pltpu.VMEM)


def in_hbm(a):
    return pltpu.with_memory_space_constraint(a, pltpu.HBM)


def dot(a, b):
    return lax.dot_general(a, b, (((1,), (0,)), ((), ())), preferred_element_type=F32)


def dot_t(a, b):
    return lax.dot_general(a, b, (((1,), (1,)), ((), ())), preferred_element_type=F32)


def inverse_kernel(pairs, spec, leg, out, coeffs, legs, store, moved, sem, out_sem):
    base = lax.axis_index("wave") * SLOTS
    window = 5

    def copies(s):
        return (
            pltpu.make_async_copy(spec.at[s], coeffs.at[s], sem.at[0, s]),
            pltpu.make_async_copy(leg.at[s], legs.at[s], sem.at[1, s]),
        )

    def start(s):
        for copy in copies(s):
            copy.start()

    for s in range(window):
        start(s)

    def step(s, carry):
        @pl.when(s + window < SLOTS)
        def _():
            start(s + window)

        for copy in copies(s):
            copy.wait()
        p = pairs[base + s]
        edge = MW - p
        parity = p & 1
        coeff = coeffs[s].reshape(2 * FLD * LV, PLEN)
        column = lax.broadcasted_iota(jnp.int32, (1, 768), 1) + 512
        first = jnp.where(column < edge, 1.0, 0.0).astype(BF16)
        second = jnp.where(column < edge, 0.0, 1.0).astype(BF16)
        middle = coeff[:, 512:1280]
        both = dot(
            jnp.concatenate([middle * first, middle * second], 0), legs[s, 512:1280, :]
        )
        last = coeff[:, 1280:1281].astype(F32) * legs[s, 1280:1281, :].astype(F32)
        halves = (both[:256] + dot(coeff[:, 0:512], legs[s, 0:512, :]), both[256:] + last)
        for h in range(2):
            e = jnp.bitwise_xor(parity, h)
            half = halves[h].astype(BF16)
            for c in range(2):
                store[2 * e + c, s] = half[c * 128 : (c + 1) * 128].reshape(FLD, LV, NLAT)
        return carry

    leave = [
        pltpu.make_async_copy(moved.at[t], out.at[:, t], out_sem.at[t]) for t in range(5)
    ]

    def swapped(tile, blocks):
        for f in range(FLD):
            value = pltpu.einshape('slj->lsj', blocks(f).reshape(8, LV, NLAT))
            moved[tile, :, :, f * NLAT : (f + 1) * NLAT] = value
        leave[tile].start()

    lax.fori_loop(0, 8, step, 0)
    for q in range(4):
        swapped(q, lambda f: store[q, 0:8, f].reshape(8 * LV, NLAT))
    lax.fori_loop(8, SLOTS, step, 0)
    swapped(
        4, lambda f: jnp.concatenate([store[q, 8 + i, f] for i in range(2) for q in range(4)], 0)
    )
    for t in range(5):
        leave[t].wait()


def inverse_legendre(pair_table, spec_in, legendre):
    return pl.pallas_call(
        inverse_kernel,
        in_specs=[pl.BlockSpec(memory_space=pltpu.SMEM)]
        + [pl.BlockSpec(memory_space=pl.ANY)] * 2,
        out_specs=pl.BlockSpec(memory_space=pl.ANY),
        out_shape=pltpu.HBM((SRC, 5, 8, FLD * NLAT), BF16),
        scratch_shapes=[
            pltpu.VMEM((SLOTS, 2, FLD, LV, PLEN), BF16),
            pltpu.VMEM((SLOTS, PLEN, NLAT), BF16),
            pltpu.VMEM((4, SLOTS, FLD, LV, NLAT), BF16),
            pltpu.VMEM((5, SRC, 8, FLD * NLAT), BF16),
            pltpu.SemaphoreType.DMA((2, SLOTS)),
            pltpu.SemaphoreType.DMA((5,)),
        ],
        compiler_params=pltpu.CompilerParams(vmem_limit_bytes=32 * MIB),
        cost_estimate=pl.CostEstimate(
            flops=6_000_000_000, bytes_accessed=17_000_000, transcendentals=0
        ),
    )(in_hbm(pair_table), in_hbm(spec_in), in_hbm(legendre))


def small_tables(pair_table):
    pairs = pair_table.reshape(SRC, SLOTS)
    pure = pairs[:, :8].reshape(1, 256)
    mixed = jnp.repeat(pairs[:, 8:10], 4, axis=1).reshape(1, 256)
    both = jnp.broadcast_to(jnp.concatenate([pure, mixed], 1), (4, 512))
    q = jnp.arange(4, dtype=jnp.int32)[:, None]
    even_odd, part = q // 2, q % 2
    column = jnp.arange(512, dtype=jnp.int32)[None, :]
    own = (column < 256) | (column % 4 == q)
    wave = jnp.where(both % 2 == even_odd, both, MW - 1 - both)
    wave = wave.reshape(2048)
    shift = jnp.broadcast_to(part * (NLON // 4), (4, 512)).reshape(2048)
    amp = jnp.where(own, F32(1.0 / math.sqrt(MW)), F32(0.0)).reshape(2048)

    def angles(index):
        return (index % NLON).astype(F32) * F32(2.0 * math.pi / NLON)

    coarse = jnp.arange(KA // 64, dtype=jnp.int32)[:, None] * 64
    fine = jnp.arange(64, dtype=jnp.int32)[:, None]
    a1 = angles(coarse * wave[None, :])
    a2 = angles(fine * wave[None, :] + shift[None, :])
    rows = (jnp.cos(a1), jnp.sin(a1), jnp.cos(a2) * amp[None, :], jnp.sin(a2) * amp[None, :])
    coarse = jnp.arange(KB // 128, dtype=jnp.int32)[None, :] * 128
    fine = jnp.arange(128, dtype=jnp.int32)[None, :]
    b1 = angles(coarse * wave[:, None])
    b2 = angles(fine * wave[:, None] + shift[:, None])
    columns = (jnp.cos(b1), jnp.sin(b1), jnp.cos(b2) * amp[:, None], jnp.sin(b2) * amp[:, None])
    return rows, columns


def table_kernel(ca, sa, cb, sb, da, ea, db, eb, leg, weight, inv, direct, weighted):
    weighted[0] = (leg[0].astype(F32) * weight[...] * math.sqrt(PLEN / NLAT)).astype(BF16)

    @pl.when(pl.program_id(0) < 4)
    def _():
        for a in range(KA // 64):
            value = ca[a : a + 1, :] * cb[...] - sa[a : a + 1, :] * sb[...]
            if a == KA // 64 - 1:
                k = lax.broadcasted_iota(jnp.int32, (64, 1), 0) + a * 64
                value = jnp.where(k <= KLAST, value, 0.0)
            inv[0, a * 64 : (a + 1) * 64, :] = value.astype(BF16)
        for a in range(KB // 128):
            value = da[:, a : a + 1] * db[...] - ea[:, a : a + 1] * eb[...]
            if a == 0 or (a + 1) * 128 > KLAST:
                k = lax.broadcasted_iota(jnp.int32, (1, 128), 1) + a * 128
                ends = (k == 0) | (k == KLAST)
                value = value * jnp.where(ends, 0.5, jnp.where(k <= KLAST, 1.0, 0.0))
            direct[0, :, a * 128 : (a + 1) * 128] = value.astype(BF16)


def all_tables(pair_table, legendre, lat_weight):
    rows, columns = small_tables(pair_table)
    group = lambda s: jnp.minimum(s, 3)
    row_specs = [pl.BlockSpec((r.shape[0], 512), lambda s: (0, group(s))) for r in rows]
    col_specs = [pl.BlockSpec((512, c.shape[1]), lambda s: (group(s), 0)) for c in columns]
    slot_spec = pl.BlockSpec((1, PLEN, NLAT), lambda s: (s, 0, 0))
    return pl.pallas_call(
        table_kernel,
        grid=(SLOTS,),
        in_specs=row_specs
        + col_specs
        + [slot_spec, pl.BlockSpec((1, NLAT), lambda s: (0, 0))],
        out_specs=[
            pl.BlockSpec((1, KA, 512), lambda s: (group(s), 0, 0)),
            pl.BlockSpec((1, 512, KB), lambda s: (group(s), 0, 0)),
            slot_spec,
        ],
        out_shape=[
            pltpu.HBM((4, KA, 512), BF16),
            pltpu.HBM((4, 512, KB), BF16),
            pltpu.HBM((SLOTS, PLEN, NLAT), BF16),
        ],
        compiler_params=pltpu.CompilerParams(vmem_limit_bytes=24 * MIB),
        cost_estimate=pl.CostEstimate(
            flops=20_000_000, bytes_accessed=26_000_000, transcendentals=0
        ),
    )(*rows, *columns, in_hbm(legendre), lat_weight.reshape(1, NLAT))


def grid_kernel(needed, wanted, recv, inv_any, direct_any, out, inv, direct, x, v, sem):
    get_inv = [
        pltpu.make_async_copy(inv_any.at[q], inv.at[q], sem.at[0, q]) for q in range(4)
    ]
    get_direct = [
        pltpu.make_async_copy(direct_any.at[q], direct.at[q], sem.at[1, q]) for q in range(4)
    ]
    for copy in get_inv + get_direct:
        copy.start()
    for t in range(5):
        for i in range(len(needed)):
            lanes = slice(i * NLAT, (i + 1) * NLAT)
            f = needed[i]
            tile = recv[:, t, :, f * NLAT : (f + 1) * NLAT].astype(F32)
            tile = tile.reshape(256, NLAT).astype(BF16)
            for q in range(4) if t == 4 else (t,):
                row = 256 if t == 4 else 0
                x[q, row : row + 256, lanes] = tile
    sums = {}
    for q in range(4):
        get_inv[q].wait()
        for i, f in enumerate(needed):
            sums[f, q] = dot(inv[q], x[q, :, i * NLAT : (i + 1) * NLAT])
    grids = {}
    for f in needed:
        ec, es, oc, os_ = [sums[f, q] for q in range(4)]
        e_plus, e_minus, o_plus, o_minus = ec + es, ec - es, oc + os_, oc - os_
        grids[f] = (e_plus + o_plus, e_minus + o_minus, e_plus - o_plus, e_minus - o_minus)
    for q in range(4):
        get_direct[q].wait()
    scale = MW / NLON
    for i, f in enumerate(wanted):
        lanes = slice(i * NLAT, (i + 1) * NLAT)
        t0, t1, t2, t3 = [g + 0.5 * g * n for g, n in zip(grids[f], grids[(f + 1) % FLD])]
        e_plus, o_plus, e_minus, o_minus = t0 + t2, t0 - t2, t1 + t3, t1 - t3
        v[0, 0:KA, lanes] = (e_plus + e_minus).astype(BF16)
        v[1, 0:KA, lanes] = (e_plus - e_minus).astype(BF16)
        v[2, 0:KA, lanes] = (o_plus + o_minus).astype(BF16)
        v[3, 0:KA, lanes] = (o_plus - o_minus).astype(BF16)
        mixed = None
        for q in range(4):
            v[q, KA:KB, lanes] = jnp.zeros((KB - KA, NLAT), BF16)
            pure = dot(direct[q, 0:256, :], v[q, :, lanes]) * scale
            out[:, q, :, lanes] = pure.reshape(SRC, 8, NLAT).astype(BF16)
            term = dot(direct[q, 256:512, :], v[q, :, lanes])
            mixed = term if mixed is None else mixed + term
        out[:, 4, :, lanes] = (mixed * scale).reshape(SRC, 8, NLAT).astype(BF16)


def grid_step(needed, wanted, received, inv, direct):
    return pl.pallas_call(
        functools.partial(grid_kernel, needed, wanted),
        in_specs=[VM] + [pl.BlockSpec(memory_space=pl.ANY)] * 2,
        out_specs=VM,
        out_shape=pltpu.HBM((SRC, 5, 8, len(wanted) * NLAT), BF16),
        scratch_shapes=[
            pltpu.VMEM((4, KA, 512), BF16),
            pltpu.VMEM((4, 512, KB), BF16),
            pltpu.VMEM((4, 512, len(needed) * NLAT), BF16),
            pltpu.VMEM((4, KB, len(wanted) * NLAT), BF16),
            pltpu.SemaphoreType.DMA((2, 4)),
        ],
        compiler_params=pltpu.CompilerParams(vmem_limit_bytes=(12 + 8 * len(wanted)) * MIB),
        cost_estimate=pl.CostEstimate(
            flops=2_000_000_000 * len(wanted), bytes_accessed=9_000_000, transcendentals=0
        ),
    )(received, in_hbm(inv), in_hbm(direct))


def unswap(recv, lanes, write):
    for t in range(5):
        moved = pltpu.einshape('lsj->slj', recv[:, t, :, lanes])
        for r in range(8):
            if t < 4:
                write(t, r, moved[r])
            else:
                write(r % 4, 8 + r // 4, moved[r])


def thermal_kernel(recv, out):
    def write(q, s, value):
        out[q, s] = value

    unswap(recv, slice(0, NLAT), write)


def thermal_rows(received):
    return pl.pallas_call(
        thermal_kernel,
        out_shape=jax.ShapeDtypeStruct((4, SLOTS, LV, NLAT), BF16),
        compiler_params=pltpu.CompilerParams(vmem_limit_bytes=16 * MIB),
        cost_estimate=pl.CostEstimate(
            flops=170_000_000, bytes_accessed=1_400_000, transcendentals=0
        ),
    )(received)


def link_kernel(matrix, r0, r1, r2, r3, o0, o1, o2, o3):
    for s in range(SLOTS):
        column = jnp.concatenate([r[s] for r in (r0, r1, r2, r3)], 0)
        result = dot(matrix[...], column).astype(BF16)
        for i, o in enumerate((o0, o1, o2, o3)):
            o[s] = result[i * LV : (i + 1) * LV]


def vertical_link(rows, vertical_matrix):
    me = lax.axis_index("lev")
    double = jnp.concatenate([vertical_matrix, vertical_matrix], 0)
    rolled = lax.dynamic_slice_in_dim(double, me * LV, 4 * LV, 0)
    double = jnp.concatenate([rolled, rolled], 1)
    rolled = lax.dynamic_slice_in_dim(double, me * LV, 4 * LV, 1)

    def moved(value, shift):
        if shift == 0:
            return value
        return lax.ppermute(value, "lev", [(i, (i + shift) % 4) for i in range(4)])

    def chunk(shift):
        return lax.dynamic_index_in_dim(rows, (me + shift) % 4, 0, keepdims=False)

    order = (1, 3, 2, 0)
    got = {shift: moved(chunk(shift), shift) for shift in order}
    relative = [got[(-i) % 4] for i in range(4)]
    shape = jax.ShapeDtypeStruct((SLOTS, LV, NLAT), BF16)
    linked = pl.pallas_call(
        link_kernel,
        out_shape=[shape] * 4,
        compiler_params=pltpu.CompilerParams(vmem_limit_bytes=16 * MIB),
        cost_estimate=pl.CostEstimate(
            flops=90_000_000, bytes_accessed=1_400_000, transcendentals=0
        ),
    )(rolled, *relative)
    back = {shift: moved(linked[shift], shift) for shift in order}
    return [back[shift] for shift in range(4)]


def edge_of(pairs, s):
    p = pairs[lax.axis_index("wave") * SLOTS + s]
    return p, MW - p, p & 1


def legendre_rows(edge, left, weighted, give, mend):
    for r0 in range(0, 1280, 256):
        half = 0 if r0 < 512 else (r0 >= edge).astype(jnp.int32)
        give(r0, 256, dot_t(left(half), weighted(r0, 256)))
    left1 = left(1)
    row = weighted(1280, 1).astype(F32)
    give(1280, 1, jnp.sum(left1.astype(F32) * row, axis=1, keepdims=True))
    r0 = pl.multiple_of(jnp.minimum(edge // 256, 4) * 256, 256)
    r = lax.broadcasted_iota(jnp.int32, (1, 256), 1) + r0
    mend(r0, r < edge, dot_t(left1, weighted(r0, 256)))


def over_slots(weight, table, sem, before, slot, leave):
    window = 4

    def arrive(s):
        return pltpu.make_async_copy(weight.at[s], table.at[s], sem.at[s])

    for s in range(window):
        arrive(s).start()
    before()

    def step(s, carry):
        @pl.when(s + window < SLOTS)
        def _():
            arrive(s + window).start()

        arrive(s).wait()
        slot(s, lambda r0, width: table[s, pl.ds(r0, width), :])
        for copy in leave(s):
            copy.start()
        return carry

    lax.fori_loop(0, SLOTS, step, 0)
    for s in range(SLOTS):
        for copy in leave(s):
            copy.wait()


def thermal_result_kernel(pairs, rows2, weight, out, table, stage, sem, out_sem):
    def leave(s):
        return [
            pltpu.make_async_copy(stage.at[s, c], out.at[s, c, 2], out_sem.at[s, c])
            for c in range(2)
        ]

    def slot(s, weighted):
        p, edge, parity = edge_of(pairs, s)

        def left(h):
            q = 2 * jnp.bitwise_xor(parity, h)
            return jnp.concatenate([rows2[q, s], rows2[q + 1, s]], 0)

        def give(r0, width, value):
            value = value.reshape(2, LV, width).astype(BF16)
            stage[s, :, :, r0 : r0 + width] = value

        def mend(r0, keep, value):
            lanes = pl.ds(r0, 256)
            value = jnp.where(keep, stage[s, :, :, lanes].astype(F32), value.reshape(2, LV, 256))
            stage[s, :, :, lanes] = value.astype(BF16)

        legendre_rows(edge, left, weighted, give, mend)

    over_slots(weight, table, sem, lambda: None, slot, leave)


def thermal_result(pair_table, rows2, weighted):
    return pl.pallas_call(
        thermal_result_kernel,
        in_specs=[
            pl.BlockSpec(memory_space=pltpu.SMEM), VM, pl.BlockSpec(memory_space=pl.ANY)
        ],
        out_specs=pl.BlockSpec(memory_space=pl.ANY),
        out_shape=jax.ShapeDtypeStruct((SLOTS, 2, FLD, LV, PLEN), BF16),
        scratch_shapes=[
            pltpu.VMEM((SLOTS, PLEN, NLAT), BF16),
            pltpu.VMEM((SLOTS, 2, LV, PLEN), BF16),
            pltpu.SemaphoreType.DMA((SLOTS,)),
            pltpu.SemaphoreType.DMA((SLOTS, 2)),
        ],
        compiler_params=pltpu.CompilerParams(vmem_limit_bytes=20 * MIB),
        cost_estimate=pl.CostEstimate(
            flops=2_000_000_000, bytes_accessed=9_000_000, transcendentals=0
        ),
    )(pair_table, rows2, in_hbm(weighted))


def rest_kernel(pairs, recv, c0, c1, c2, c3, weight, begun, out, store, table, stage, sem, out_sem):
    def before():
        me = lax.axis_index("lev")
        for shift, c in enumerate((c0, c1, c2, c3)):
            store[3, lax.rem(me - shift + 4, 4)] = c[...]
        for place in range(3):
            def write(q, slot, value):
                store[place, q, slot] = value

            unswap(recv, slice(place * NLAT, (place + 1) * NLAT), write)

    def leave(s):
        return [
            pltpu.make_async_copy(
                stage.at[s, c, pl.ds(0, 2)], out.at[s, c, pl.ds(0, 2)], out_sem.at[s, c, 0]
            )
            for c in range(2)
        ] + [
            pltpu.make_async_copy(stage.at[s, c, 2], out.at[s, c, 3], out_sem.at[s, c, 1])
            for c in range(2)
        ]

    def slot(s, weighted):
        p, edge, parity = edge_of(pairs, s)

        def left(h):
            q = 2 * jnp.bitwise_xor(parity, h)
            return jnp.concatenate([store[f, q + c, s] for c in range(2) for f in range(4)], 0)

        def corrected(r0, width, value):
            r = lax.broadcasted_iota(jnp.int32, (1, width), 1) + r0
            degree = jnp.where(r < edge, p + r, r - 1).astype(F32)
            implicit = degree * (degree + 1.0) / float(MW * (MW - 1))
            value = value.reshape(2, 4, LV, width)
            return [
                [value[c, 0] - implicit * value[c, 3], value[c, 1], value[c, 2]] for c in range(2)
            ]

        def give(r0, width, value):
            for c, fields in enumerate(corrected(r0, width, value)):
                for f in range(3):
                    stage[s, c, f, :, r0 : r0 + width] = fields[f].astype(BF16)

        def mend(r0, keep, value):
            lanes = pl.ds(r0, 256)
            for c, fields in enumerate(corrected(r0, 256, value)):
                for f in range(3):
                    kept = stage[s, c, f, :, lanes].astype(F32)
                    stage[s, c, f, :, lanes] = jnp.where(keep, kept, fields[f]).astype(BF16)

        legendre_rows(edge, left, weighted, give, mend)

    over_slots(weight, table, sem, before, slot, leave)


def rest_result(pair_table, received, coupled, weighted, begun):
    return pl.pallas_call(
        rest_kernel,
        in_specs=[pl.BlockSpec(memory_space=pltpu.SMEM)]
        + [VM] * 5
        + [pl.BlockSpec(memory_space=pl.ANY)] * 2,
        out_specs=pl.BlockSpec(memory_space=pl.ANY),
        out_shape=jax.ShapeDtypeStruct((SLOTS, 2, FLD, LV, PLEN), BF16),
        input_output_aliases={7: 0},
        scratch_shapes=[
            pltpu.VMEM((4, 4, SLOTS, LV, NLAT), BF16),
            pltpu.VMEM((SLOTS, PLEN, NLAT), BF16),
            pltpu.VMEM((SLOTS, 2, 3, LV, PLEN), BF16),
            pltpu.SemaphoreType.DMA((SLOTS,)),
            pltpu.SemaphoreType.DMA((SLOTS, 2, 2)),
        ],
        compiler_params=pltpu.CompilerParams(vmem_limit_bytes=24 * MIB),
        cost_estimate=pl.CostEstimate(
            flops=5_000_000_000, bytes_accessed=15_000_000, transcendentals=0
        ),
    )(pair_table, received, *coupled, in_hbm(weighted), in_hbm(begun))


def exchange(value):
    return lax.all_to_all(value, "wave", split_axis=0, concat_axis=0, tiled=True)


def local(spec_in, legendre, lat_weight, vertical_matrix, pair_table):
    sent = inverse_legendre(pair_table, spec_in, legendre)
    received = exchange(sent)
    inv, direct, weighted = all_tables(pair_table, legendre, lat_weight)
    arrived2 = exchange(grid_step((2, 3), (2,), received, inv, direct))
    arrived_rest = exchange(grid_step((0, 1, 2, 3), (0, 1, 3), received, inv, direct))
    rows2 = thermal_rows(arrived2)
    coupled = vertical_link(rows2, vertical_matrix)
    begun = thermal_result(pair_table, rows2, weighted)
    return rest_result(pair_table, arrived_rest, coupled, weighted, begun)


def solution(mesh):
    return jax.shard_map(
        local,
        mesh=mesh,
        in_specs=(P("wave", None, None, "lev", None), P("wave", None, None), P(), P(), P()),
        out_specs=P("wave", None, None, "lev", None),
        check_vma=False,
    )
```

```python
import functools
import math

import jax
import jax.numpy as jnp
from jax import lax
from jax.experimental import pallas as pl
from jax.experimental.pallas import tpu as pltpu
from jax.sharding import PartitionSpec as P

MW = 1280
NLON = 2688
FLD = 4
PLEN = 1281
NLAT = 256
SLOTS = 10
LV = 32
SRC = 32
KA = 704
KB = 768
KLAST = 672
F32 = jnp.float32
BF16 = jnp.bfloat16
MIB = 1024 * 1024
VM = pl.BlockSpec(memory_space=pltpu.VMEM)


def in_hbm(a):
    return pltpu.with_memory_space_constraint(a, pltpu.HBM)


def dot(a, b):
    return lax.dot_general(a, b, (((1,), (0,)), ((), ())), preferred_element_type=F32)


def dot_t(a, b):
    return lax.dot_general(a, b, (((1,), (1,)), ((), ())), preferred_element_type=F32)


def inverse_kernel(pairs, spec, leg, out, coeffs, legs, store, moved, sem, out_sem):
    base = lax.axis_index("wave") * SLOTS
    window = 5

    def copies(s):
        return (
            pltpu.make_async_copy(spec.at[s], coeffs.at[s], sem.at[0, s]),
            pltpu.make_async_copy(leg.at[s], legs.at[s], sem.at[1, s]),
        )

    def start(s):
        for copy in copies(s):
            copy.start()

    for s in range(window):
        start(s)

    def step(s, carry):
        @pl.when(s + window < SLOTS)
        def _():
            start(s + window)

        for copy in copies(s):
            copy.wait()
        p = pairs[base + s]
        edge = MW - p
        parity = p & 1
        coeff = coeffs[s].reshape(2 * FLD * LV, PLEN)
        column = lax.broadcasted_iota(jnp.int32, (1, 768), 1) + 512
        first = jnp.where(column < edge, 1.0, 0.0).astype(BF16)
        second = jnp.where(column < edge, 0.0, 1.0).astype(BF16)
        middle = coeff[:, 512:1280]
        both = dot(
            jnp.concatenate([middle * first, middle * second], 0), legs[s, 512:1280, :]
        )
        last = coeff[:, 1280:1281].astype(F32) * legs[s, 1280:1281, :].astype(F32)
        halves = (both[:256] + dot(coeff[:, 0:512], legs[s, 0:512, :]), both[256:] + last)
        for h in range(2):
            e = jnp.bitwise_xor(parity, h)
            half = halves[h].astype(BF16)
            for c in range(2):
                store[2 * e + c, s] = half[c * 128 : (c + 1) * 128].reshape(FLD, LV, NLAT)
        return carry

    leave = [
        pltpu.make_async_copy(moved.at[t], out.at[:, t], out_sem.at[t]) for t in range(5)
    ]

    def swapped(tile, blocks):
        for f in range(FLD):
            value = pltpu.einshape('slj->lsj', blocks(f).reshape(8, LV, NLAT))
            moved[tile, :, :, f * NLAT : (f + 1) * NLAT] = value
        leave[tile].start()

    lax.fori_loop(0, 8, step, 0)
    for q in range(4):
        swapped(q, lambda f: store[q, 0:8, f].reshape(8 * LV, NLAT))
    lax.fori_loop(8, SLOTS, step, 0)
    swapped(
        4, lambda f: jnp.concatenate([store[q, 8 + i, f] for i in range(2) for q in range(4)], 0)
    )
    for t in range(5):
        leave[t].wait()


def inverse_legendre(pair_table, spec_in, legendre):
    return pl.pallas_call(
        inverse_kernel,
        in_specs=[pl.BlockSpec(memory_space=pltpu.SMEM)]
        + [pl.BlockSpec(memory_space=pl.ANY)] * 2,
        out_specs=pl.BlockSpec(memory_space=pl.ANY),
        out_shape=pltpu.HBM((SRC, 5, 8, FLD * NLAT), BF16),
        scratch_shapes=[
            pltpu.VMEM((SLOTS, 2, FLD, LV, PLEN), BF16),
            pltpu.VMEM((SLOTS, PLEN, NLAT), BF16),
            pltpu.VMEM((4, SLOTS, FLD, LV, NLAT), BF16),
            pltpu.VMEM((5, SRC, 8, FLD * NLAT), BF16),
            pltpu.SemaphoreType.DMA((2, SLOTS)),
            pltpu.SemaphoreType.DMA((5,)),
        ],
        compiler_params=pltpu.CompilerParams(vmem_limit_bytes=32 * MIB),
        cost_estimate=pl.CostEstimate(
            flops=6_000_000_000, bytes_accessed=17_000_000, transcendentals=0
        ),
    )(in_hbm(pair_table), in_hbm(spec_in), in_hbm(legendre))


def small_tables(pair_table):
    pairs = pair_table.reshape(SRC, SLOTS)
    pure = pairs[:, :8].reshape(1, 256)
    mixed = jnp.repeat(pairs[:, 8:10], 4, axis=1).reshape(1, 256)
    both = jnp.broadcast_to(jnp.concatenate([pure, mixed], 1), (4, 512))
    q = jnp.arange(4, dtype=jnp.int32)[:, None]
    even_odd, part = q // 2, q % 2
    column = jnp.arange(512, dtype=jnp.int32)[None, :]
    own = (column < 256) | (column % 4 == q)
    wave = jnp.where(both % 2 == even_odd, both, MW - 1 - both)
    wave = wave.reshape(2048)
    shift = jnp.broadcast_to(part * (NLON // 4), (4, 512)).reshape(2048)
    amp = jnp.where(own, F32(1.0 / math.sqrt(MW)), F32(0.0)).reshape(2048)

    def angles(index):
        return (index % NLON).astype(F32) * F32(2.0 * math.pi / NLON)

    coarse = jnp.arange(KA // 64, dtype=jnp.int32)[:, None] * 64
    fine = jnp.arange(64, dtype=jnp.int32)[:, None]
    a1 = angles(coarse * wave[None, :])
    a2 = angles(fine * wave[None, :] + shift[None, :])
    rows = (jnp.cos(a1), jnp.sin(a1), jnp.cos(a2) * amp[None, :], jnp.sin(a2) * amp[None, :])
    coarse = jnp.arange(KB // 128, dtype=jnp.int32)[None, :] * 128
    fine = jnp.arange(128, dtype=jnp.int32)[None, :]
    b1 = angles(coarse * wave[:, None])
    b2 = angles(fine * wave[:, None] + shift[:, None])
    columns = (jnp.cos(b1), jnp.sin(b1), jnp.cos(b2) * amp[:, None], jnp.sin(b2) * amp[:, None])
    return rows, columns


def table_kernel(ca, sa, cb, sb, da, ea, db, eb, leg, weight, inv, direct, weighted):
    weighted[0] = (leg[0].astype(F32) * weight[...] * math.sqrt(PLEN / NLAT)).astype(BF16)

    @pl.when(pl.program_id(0) < 4)
    def _():
        for a in range(KA // 64):
            value = ca[a : a + 1, :] * cb[...] - sa[a : a + 1, :] * sb[...]
            if a == KA // 64 - 1:
                k = lax.broadcasted_iota(jnp.int32, (64, 1), 0) + a * 64
                value = jnp.where(k <= KLAST, value, 0.0)
            inv[0, a * 64 : (a + 1) * 64, :] = value.astype(BF16)
        for a in range(KB // 128):
            value = da[:, a : a + 1] * db[...] - ea[:, a : a + 1] * eb[...]
            if a == 0 or (a + 1) * 128 > KLAST:
                k = lax.broadcasted_iota(jnp.int32, (1, 128), 1) + a * 128
                ends = (k == 0) | (k == KLAST)
                value = value * jnp.where(ends, 0.5, jnp.where(k <= KLAST, 1.0, 0.0))
            direct[0, :, a * 128 : (a + 1) * 128] = value.astype(BF16)


def all_tables(pair_table, legendre, lat_weight):
    rows, columns = small_tables(pair_table)
    group = lambda s: jnp.minimum(s, 3)
    row_specs = [pl.BlockSpec((r.shape[0], 512), lambda s: (0, group(s))) for r in rows]
    col_specs = [pl.BlockSpec((512, c.shape[1]), lambda s: (group(s), 0)) for c in columns]
    slot_spec = pl.BlockSpec((1, PLEN, NLAT), lambda s: (s, 0, 0))
    return pl.pallas_call(
        table_kernel,
        grid=(SLOTS,),
        in_specs=row_specs
        + col_specs
        + [slot_spec, pl.BlockSpec((1, NLAT), lambda s: (0, 0))],
        out_specs=[
            pl.BlockSpec((1, KA, 512), lambda s: (group(s), 0, 0)),
            pl.BlockSpec((1, 512, KB), lambda s: (group(s), 0, 0)),
            slot_spec,
        ],
        out_shape=[
            pltpu.HBM((4, KA, 512), BF16),
            pltpu.HBM((4, 512, KB), BF16),
            pltpu.HBM((SLOTS, PLEN, NLAT), BF16),
        ],
        compiler_params=pltpu.CompilerParams(vmem_limit_bytes=24 * MIB),
        cost_estimate=pl.CostEstimate(
            flops=20_000_000, bytes_accessed=26_000_000, transcendentals=0
        ),
    )(*rows, *columns, in_hbm(legendre), lat_weight.reshape(1, NLAT))


def grid_kernel(needed, wanted, recv, inv_any, direct_any, out, inv, direct, x, v, stage, sem, out_sem):
    get_inv = [
        pltpu.make_async_copy(inv_any.at[q], inv.at[q], sem.at[0, q]) for q in range(4)
    ]
    get_direct = [
        pltpu.make_async_copy(direct_any.at[q], direct.at[q], sem.at[1, q]) for q in range(4)
    ]
    leave = [
        pltpu.make_async_copy(
            stage.at[:, :, :, pl.ds(i * NLAT, NLAT)],
            out.at[:, :, :, pl.ds(i * NLAT, NLAT)],
            out_sem.at[i],
        )
        for i in range(len(wanted))
    ]
    for copy in get_inv + get_direct:
        copy.start()
    for t in range(5):
        for i in range(len(needed)):
            lanes = slice(i * NLAT, (i + 1) * NLAT)
            f = needed[i]
            tile = recv[:, t, :, f * NLAT : (f + 1) * NLAT].astype(F32)
            tile = tile.reshape(256, NLAT).astype(BF16)
            for q in range(4) if t == 4 else (t,):
                row = 256 if t == 4 else 0
                x[q, row : row + 256, lanes] = tile
    sums = {}
    for q in range(4):
        get_inv[q].wait()
    for q in range(4):
        for i, f in enumerate(needed):
            sums[f, q] = dot(inv[q], x[q, :, i * NLAT : (i + 1) * NLAT])
    grids = {}
    for f in needed:
        ec, es, oc, os_ = [sums[f, q] for q in range(4)]
        e_plus, e_minus, o_plus, o_minus = ec + es, ec - es, oc + os_, oc - os_
        grids[f] = (e_plus + o_plus, e_minus + o_minus, e_plus - o_plus, e_minus - o_minus)
    for q in range(4):
        get_direct[q].wait()
    scale = MW / NLON
    for i, f in enumerate(wanted):
        lanes = slice(i * NLAT, (i + 1) * NLAT)
        t0, t1, t2, t3 = [g + 0.5 * g * n for g, n in zip(grids[f], grids[(f + 1) % FLD])]
        e_plus, o_plus, e_minus, o_minus = t0 + t2, t0 - t2, t1 + t3, t1 - t3
        v[0, 0:KA, lanes] = (e_plus + e_minus).astype(BF16)
        v[1, 0:KA, lanes] = (e_plus - e_minus).astype(BF16)
        v[2, 0:KA, lanes] = (o_plus + o_minus).astype(BF16)
        v[3, 0:KA, lanes] = (o_plus - o_minus).astype(BF16)
        mixed = None
        for q in range(4):
            v[q, KA:KB, lanes] = jnp.zeros((KB - KA, NLAT), BF16)
            pure = dot(direct[q, 0:256, :], v[q, :, lanes]) * scale
            stage[:, q, :, lanes] = pure.reshape(SRC, 8, NLAT).astype(BF16)
            term = dot(direct[q, 256:512, :], v[q, :, lanes])
            mixed = term if mixed is None else mixed + term
        stage[:, 4, :, lanes] = (mixed * scale).reshape(SRC, 8, NLAT).astype(BF16)
        leave[i].start()
    for copy in leave:
        copy.wait()


def grid_step(needed, wanted, received, inv, direct):
    return pl.pallas_call(
        functools.partial(grid_kernel, needed, wanted),
        in_specs=[VM] + [pl.BlockSpec(memory_space=pl.ANY)] * 2,
        out_specs=pl.BlockSpec(memory_space=pl.ANY),
        out_shape=pltpu.HBM((SRC, 5, 8, len(wanted) * NLAT), BF16),
        scratch_shapes=[
            pltpu.VMEM((4, KA, 512), BF16),
            pltpu.VMEM((4, 512, KB), BF16),
            pltpu.VMEM((4, 512, len(needed) * NLAT), BF16),
            pltpu.VMEM((4, KB, len(wanted) * NLAT), BF16),
            pltpu.VMEM((SRC, 5, 8, len(wanted) * NLAT), BF16),
            pltpu.SemaphoreType.DMA((2, 4)),
            pltpu.SemaphoreType.DMA((len(wanted),)),
        ],
        compiler_params=pltpu.CompilerParams(vmem_limit_bytes=(12 + 8 * len(wanted)) * MIB),
        cost_estimate=pl.CostEstimate(
            flops=2_000_000_000 * len(wanted), bytes_accessed=9_000_000, transcendentals=0
        ),
    )(received, in_hbm(inv), in_hbm(direct))


def unswap(recv, lanes, write):
    for t in range(5):
        moved = pltpu.einshape('lsj->slj', recv[:, t, :, lanes])
        for r in range(8):
            if t < 4:
                write(t, r, moved[r])
            else:
                write(r % 4, 8 + r // 4, moved[r])


def thermal_kernel(recv, out):
    def write(q, s, value):
        out[q, s] = value

    unswap(recv, slice(0, NLAT), write)


def thermal_rows(received):
    return pl.pallas_call(
        thermal_kernel,
        out_shape=jax.ShapeDtypeStruct((4, SLOTS, LV, NLAT), BF16),
        compiler_params=pltpu.CompilerParams(vmem_limit_bytes=16 * MIB),
        cost_estimate=pl.CostEstimate(
            flops=170_000_000, bytes_accessed=1_400_000, transcendentals=0
        ),
    )(received)


def link_kernel(matrix, r0, r1, r2, r3, o0, o1, o2, o3):
    for s in range(SLOTS):
        column = jnp.concatenate([r[s] for r in (r0, r1, r2, r3)], 0)
        result = dot(matrix[...], column).astype(BF16)
        for i, o in enumerate((o0, o1, o2, o3)):
            o[s] = result[i * LV : (i + 1) * LV]


def vertical_link(rows, vertical_matrix):
    me = lax.axis_index("lev")
    double = jnp.concatenate([vertical_matrix, vertical_matrix], 0)
    rolled = lax.dynamic_slice_in_dim(double, me * LV, 4 * LV, 0)
    double = jnp.concatenate([rolled, rolled], 1)
    rolled = lax.dynamic_slice_in_dim(double, me * LV, 4 * LV, 1)

    def moved(value, shift):
        if shift == 0:
            return value
        return lax.ppermute(value, "lev", [(i, (i + shift) % 4) for i in range(4)])

    def chunk(shift):
        return lax.dynamic_index_in_dim(rows, (me + shift) % 4, 0, keepdims=False)

    order = (1, 3, 2, 0)
    got = {shift: moved(chunk(shift), shift) for shift in order}
    relative = [got[(-i) % 4] for i in range(4)]
    shape = jax.ShapeDtypeStruct((SLOTS, LV, NLAT), BF16)
    linked = pl.pallas_call(
        link_kernel,
        out_shape=[shape] * 4,
        compiler_params=pltpu.CompilerParams(vmem_limit_bytes=16 * MIB),
        cost_estimate=pl.CostEstimate(
            flops=90_000_000, bytes_accessed=1_400_000, transcendentals=0
        ),
    )(rolled, *relative)
    back = {shift: moved(linked[shift], shift) for shift in order}
    return [back[shift] for shift in range(4)]


def edge_of(pairs, s):
    p = pairs[lax.axis_index("wave") * SLOTS + s]
    return p, MW - p, p & 1


def legendre_rows(edge, left, weighted, give, mend):
    for r0 in range(0, 1280, 256):
        half = 0 if r0 < 512 else (r0 >= edge).astype(jnp.int32)
        give(r0, 256, dot_t(left(half), weighted(r0, 256)))
    left1 = left(1)
    row = weighted(1280, 1).astype(F32)
    give(1280, 1, jnp.sum(left1.astype(F32) * row, axis=1, keepdims=True))
    r0 = pl.multiple_of(jnp.minimum(edge // 256, 4) * 256, 256)
    r = lax.broadcasted_iota(jnp.int32, (1, 256), 1) + r0
    mend(r0, r < edge, dot_t(left1, weighted(r0, 256)))


def over_slots(weight, table, sem, before, slot, leave):
    window = 4

    def arrive(s):
        return pltpu.make_async_copy(weight.at[s], table.at[s], sem.at[s])

    for s in range(window):
        arrive(s).start()
    before()

    def step(s, carry):
        @pl.when(s + window < SLOTS)
        def _():
            arrive(s + window).start()

        arrive(s).wait()
        slot(s, lambda r0, width: table[s, pl.ds(r0, width), :])
        for copy in leave(s):
            copy.start()
        return carry

    lax.fori_loop(0, SLOTS, step, 0)
    for s in range(SLOTS):
        for copy in leave(s):
            copy.wait()


def thermal_result_kernel(pairs, rows2, weight, out, table, stage, sem, out_sem):
    def leave(s):
        return [
            pltpu.make_async_copy(stage.at[s, c], out.at[s, c, 2], out_sem.at[s, c])
            for c in range(2)
        ]

    def slot(s, weighted):
        p, edge, parity = edge_of(pairs, s)

        def left(h):
            q = 2 * jnp.bitwise_xor(parity, h)
            return jnp.concatenate([rows2[q, s], rows2[q + 1, s]], 0)

        def give(r0, width, value):
            value = value.reshape(2, LV, width).astype(BF16)
            stage[s, :, :, r0 : r0 + width] = value

        def mend(r0, keep, value):
            lanes = pl.ds(r0, 256)
            value = jnp.where(keep, stage[s, :, :, lanes].astype(F32), value.reshape(2, LV, 256))
            stage[s, :, :, lanes] = value.astype(BF16)

        legendre_rows(edge, left, weighted, give, mend)

    over_slots(weight, table, sem, lambda: None, slot, leave)


def thermal_result(pair_table, rows2, weighted):
    return pl.pallas_call(
        thermal_result_kernel,
        in_specs=[
            pl.BlockSpec(memory_space=pltpu.SMEM), VM, pl.BlockSpec(memory_space=pl.ANY)
        ],
        out_specs=pl.BlockSpec(memory_space=pl.ANY),
        out_shape=jax.ShapeDtypeStruct((SLOTS, 2, FLD, LV, PLEN), BF16),
        scratch_shapes=[
            pltpu.VMEM((SLOTS, PLEN, NLAT), BF16),
            pltpu.VMEM((SLOTS, 2, LV, PLEN), BF16),
            pltpu.SemaphoreType.DMA((SLOTS,)),
            pltpu.SemaphoreType.DMA((SLOTS, 2)),
        ],
        compiler_params=pltpu.CompilerParams(vmem_limit_bytes=20 * MIB),
        cost_estimate=pl.CostEstimate(
            flops=2_000_000_000, bytes_accessed=9_000_000, transcendentals=0
        ),
    )(pair_table, rows2, in_hbm(weighted))


def rest_kernel(pairs, recv, c0, c1, c2, c3, weight, begun, out, store, table, stage, sem, out_sem):
    def before():
        me = lax.axis_index("lev")
        for shift, c in enumerate((c0, c1, c2, c3)):
            store[3, lax.rem(me - shift + 4, 4)] = c[...]
        for place in range(3):
            def write(q, slot, value):
                store[place, q, slot] = value

            unswap(recv, slice(place * NLAT, (place + 1) * NLAT), write)

    def leave(s):
        return [
            pltpu.make_async_copy(
                stage.at[s, c, pl.ds(0, 2)], out.at[s, c, pl.ds(0, 2)], out_sem.at[s, c, 0]
            )
            for c in range(2)
        ] + [
            pltpu.make_async_copy(stage.at[s, c, 2], out.at[s, c, 3], out_sem.at[s, c, 1])
            for c in range(2)
        ]

    def slot(s, weighted):
        p, edge, parity = edge_of(pairs, s)

        def left(h):
            q = 2 * jnp.bitwise_xor(parity, h)
            return jnp.concatenate([store[f, q + c, s] for c in range(2) for f in range(4)], 0)

        def corrected(r0, width, value):
            r = lax.broadcasted_iota(jnp.int32, (1, width), 1) + r0
            degree = jnp.where(r < edge, p + r, r - 1).astype(F32)
            implicit = degree * (degree + 1.0) / float(MW * (MW - 1))
            value = value.reshape(2, 4, LV, width)
            return [
                [value[c, 0] - implicit * value[c, 3], value[c, 1], value[c, 2]] for c in range(2)
            ]

        def give(r0, width, value):
            for c, fields in enumerate(corrected(r0, width, value)):
                for f in range(3):
                    stage[s, c, f, :, r0 : r0 + width] = fields[f].astype(BF16)

        def mend(r0, keep, value):
            lanes = pl.ds(r0, 256)
            for c, fields in enumerate(corrected(r0, 256, value)):
                for f in range(3):
                    kept = stage[s, c, f, :, lanes].astype(F32)
                    stage[s, c, f, :, lanes] = jnp.where(keep, kept, fields[f]).astype(BF16)

        legendre_rows(edge, left, weighted, give, mend)

    over_slots(weight, table, sem, before, slot, leave)


def rest_result(pair_table, received, coupled, weighted, begun):
    return pl.pallas_call(
        rest_kernel,
        in_specs=[pl.BlockSpec(memory_space=pltpu.SMEM)]
        + [VM] * 5
        + [pl.BlockSpec(memory_space=pl.ANY)] * 2,
        out_specs=pl.BlockSpec(memory_space=pl.ANY),
        out_shape=jax.ShapeDtypeStruct((SLOTS, 2, FLD, LV, PLEN), BF16),
        input_output_aliases={7: 0},
        scratch_shapes=[
            pltpu.VMEM((4, 4, SLOTS, LV, NLAT), BF16),
            pltpu.VMEM((SLOTS, PLEN, NLAT), BF16),
            pltpu.VMEM((SLOTS, 2, 3, LV, PLEN), BF16),
            pltpu.SemaphoreType.DMA((SLOTS,)),
            pltpu.SemaphoreType.DMA((SLOTS, 2, 2)),
        ],
        compiler_params=pltpu.CompilerParams(vmem_limit_bytes=24 * MIB),
        cost_estimate=pl.CostEstimate(
            flops=5_000_000_000, bytes_accessed=15_000_000, transcendentals=0
        ),
    )(pair_table, received, *coupled, in_hbm(weighted), in_hbm(begun))


def exchange(value):
    return lax.all_to_all(value, "wave", split_axis=0, concat_axis=0, tiled=True)


def local(spec_in, legendre, lat_weight, vertical_matrix, pair_table):
    sent = inverse_legendre(pair_table, spec_in, legendre)
    received = exchange(sent)
    inv, direct, weighted = all_tables(pair_table, legendre, lat_weight)
    arrived2 = exchange(grid_step((2, 3), (2,), received, inv, direct))
    arrived_rest = exchange(grid_step((0, 1, 2, 3), (0, 1, 3), received, inv, direct))
    rows2 = thermal_rows(arrived2)
    coupled = vertical_link(rows2, vertical_matrix)
    begun = thermal_result(pair_table, rows2, weighted)
    return rest_result(pair_table, arrived_rest, coupled, weighted, begun)


def solution(mesh):
    return jax.shard_map(
        local,
        mesh=mesh,
        in_specs=(P("wave", None, None, "lev", None), P("wave", None, None), P(), P(), P()),
        out_specs=P("wave", None, None, "lev", None),
        check_vma=False,
    )
```
